32 devices in a mesh: seq: 4 (over y, x), fsdp: 8 (over z, core).
Axes of the slice: x: 2, y: 2, z: 4, core: 2. Of those that a mesh axis runs over, the one named last changes fastest.
Arguments:
- tokens: bfloat16 [32768, 640], P(('seq', 'fsdp')), may hold values from -6 to 6
- segment_ids: int32 [32768], P(('seq', 'fsdp')), may hold values from 0 to 4, as said below
- positions: int32 [32768], P(('seq', 'fsdp')), may hold values from 0 to 8191, as said below
- query_weight: bfloat16 [640, 1024], P('fsdp'), may hold values from -0.25 to 0.25
- key_weight: bfloat16 [640, 256], P('fsdp'), may hold values from -0.25 to 0.25
- value_weight: bfloat16 [640, 256], P('fsdp'), may hold values from -0.25 to 0.25
- out_weight: bfloat16 [1024, 640], P('fsdp'), may hold values from -0.1875 to 0.1875
- gate_weight: bfloat16 [640, 2048], P('fsdp'), may hold values from -0.25 to 0.25
- up_weight: bfloat16 [640, 2048], P('fsdp'), may hold values from -0.25 to 0.25
- down_weight: bfloat16 [2048, 640], P('fsdp'), may hold values from -0.125 to 0.125
- gain_in: bfloat16 [640], P('fsdp'), may hold values from 0.25 to 1.75
- gain_query: bfloat16 [256], P('fsdp'), may hold values from 0.25 to 1.75
- gain_key: bfloat16 [256], P('fsdp'), may hold values from 0.25 to 1.75
- gain_attn: bfloat16 [640], P('fsdp'), may hold values from 0.25 to 1.75
- gain_pre: bfloat16 [640], P('fsdp'), may hold values from 0.25 to 1.75
- gain_ffn: bfloat16 [640], P('fsdp'), may hold values from 0.25 to 1.75
- cotangent: bfloat16 [32768, 640], P(('seq', 'fsdp')), may hold values from -6 to 6
Outputs:
- output: bfloat16 [32768, 640], P(('seq', 'fsdp'))
- grad_tokens: float32 [32768, 640], P(('seq', 'fsdp'))
- grad_query_weight: float32 [640, 1024], P('fsdp')
- grad_key_weight: float32 [640, 256], P('fsdp')
- grad_value_weight: float32 [640, 256], P('fsdp')
- grad_out_weight: float32 [1024, 640], P('fsdp')
- grad_gate_weight: float32 [640, 2048], P('fsdp')
- grad_up_weight: float32 [640, 2048], P('fsdp')
- grad_down_weight: float32 [2048, 640], P('fsdp')
- grad_gain_in: float32 [640], P('fsdp')
- grad_gain_query: float32 [256], P('fsdp')
- grad_gain_key: float32 [256], P('fsdp')
- grad_gain_attn: float32 [640], P('fsdp')
- grad_gain_pre: float32 [640], P('fsdp')
- grad_gain_ffn: float32 [640], P('fsdp')
The draws below stay inside these ranges and needn't reach their ends.
Inputs may be any that keep to these rules, and one draw needn't show every extreme that they name: `segment_ids`: token t is in segment (t + r) // 8192 for one r of 1 to 1023 that the case draws: segments are contiguous runs of 8192 tokens, the first and the last shorter. `positions`: A token's position counts from 0 at the first token of its segment.
All inputs are finite; a program needn't handle non-finite values.
Results may differ from the reference program's by a relative error of at most 0.025.
Values may be sent and summed in bfloat16 or wider, within the bound.
A program may use at most 192 MiB of HBM per device.

```python
import jax
import jax.numpy as jnp
from jax import lax

D = 640
HEADS = 4
HEAD = 256
FF = 2048
WINDOW = 512
SEQ = 8192
TOK_DEV = 1024
TOKENS = 32768


def segment_layout(key):
    offset = jax.random.randint(key, (), 1, TOK_DEV, dtype=jnp.int32)
    places = jnp.arange(TOKENS, dtype=jnp.int32)
    numbers = (places + offset) // SEQ
    starts = jnp.maximum(numbers * SEQ - offset, 0)
    return (numbers, places - starts)


def draw_segment_ids(key, part):
    numbers, places = segment_layout(key)
    return numbers


def draw_positions(key, part):
    numbers, places = segment_layout(key)
    return places


def level_of(rng, shape, split, least, largest):
    loudness, own = 1.0, jax.random.fold_in(rng, 6)
    for dim, shards_of in split:
        draws = jnp.exp(jax.random.uniform(jax.random.fold_in(own, dim), (shards_of,), jnp.float32, least / len(split), largest / len(split)))
        loudness = loudness * jnp.repeat(draws, shape[dim] // shards_of).reshape([-1 if axis == dim else 1 for axis in range(len(shape))])
    return loudness


def gaussian(rng, dims, scale, reach, split=(), held_as=jnp.bfloat16):
    loudness = level_of(rng, dims, split, -0.22, 0.18) if split else 1.0
    drawn = jax.random.normal(rng, dims, jnp.float32) * scale * loudness
    return jnp.minimum(jnp.maximum(drawn, -reach), reach).astype(held_as)


def setup_inputs(seed: int = 0) -> dict:
    splits = jax.random.split(jax.random.key(seed), 18)
    return {
        "tokens": gaussian(splits[0], (TOKENS, D), 1.0, 6.0, ((0, 32),)),
        "segment_ids": draw_segment_ids(jax.random.fold_in(splits[17], 71), 0),
        "positions": draw_positions(jax.random.fold_in(splits[17], 71), 0),
        "query_weight": gaussian(splits[3], (D, HEADS * HEAD), D ** -0.5, 0.25, ((0, 8),)),
        "key_weight": gaussian(splits[4], (D, HEAD), D ** -0.5, 0.25, ((0, 8),)),
        "value_weight": gaussian(splits[5], (D, HEAD), D ** -0.5, 0.25, ((0, 8),)),
        "out_weight": gaussian(splits[6], (HEADS * HEAD, D), (HEADS * HEAD) ** -0.5, 0.1875, ((0, 8),)),
        "gate_weight": gaussian(splits[7], (D, FF), D ** -0.5, 0.25, ((0, 8),)),
        "up_weight": gaussian(splits[8], (D, FF), D ** -0.5, 0.25, ((0, 8),)),
        "down_weight": gaussian(splits[9], (FF, D), FF ** -0.5, 0.125, ((0, 8),)),
        "gain_in": jnp.clip(1.0 + 0.15 * jax.random.normal(splits[10], (D,), jnp.float32), 0.25, 1.75).astype(jnp.bfloat16),
        "gain_query": jnp.clip(1.0 + 0.15 * jax.random.normal(splits[11], (HEAD,), jnp.float32), 0.25, 1.75).astype(jnp.bfloat16),
        "gain_key": jnp.clip(1.0 + 0.15 * jax.random.normal(splits[12], (HEAD,), jnp.float32), 0.25, 1.75).astype(jnp.bfloat16),
        "gain_attn": jnp.clip(1.0 + 0.15 * jax.random.normal(splits[13], (D,), jnp.float32), 0.25, 1.75).astype(jnp.bfloat16),
        "gain_pre": jnp.clip(1.0 + 0.15 * jax.random.normal(splits[14], (D,), jnp.float32), 0.25, 1.75).astype(jnp.bfloat16),
        "gain_ffn": jnp.clip(1.0 + 0.15 * jax.random.normal(splits[15], (D,), jnp.float32), 0.25, 1.75).astype(jnp.bfloat16),
        "cotangent": gaussian(splits[16], (TOKENS, D), 1.0, 6.0, ((0, 32),)),
    }


@jax.custom_vjp
def low(v):
    return lax.optimization_barrier(v.astype(jnp.bfloat16)).astype(jnp.float32)

@jax.custom_vjp
def low_back(v):
    return v

def low_keep(v):
    return (low(v), None)

def low_pass(kept, grad):
    return (grad,)

def back_keep(v):
    return (v, None)

def back_low(kept, grad):
    return (low(grad),)
low.defvjp(low_keep, low_pass)
low_back.defvjp(back_keep, back_low)
EPS = 1e-06
BASE = 10000.0
NEGATIVE = -1e+30

def rms_unit(entries):
    return entries * lax.rsqrt(lax.optimization_barrier(jnp.mean(entries * entries, axis=-1, keepdims=True)) + EPS)

def rotate(entries, cosine, sine):
    half_size = entries.shape[-1] // 2
    first = entries[..., :half_size]
    second = entries[..., half_size:]
    return jnp.concatenate([first * cosine - second * sine, second * cosine + first * sine], axis=-1)

def band_attention(query, keys, values, segment_ids):
    highest = lax.Precision.HIGHEST
    total_rows = query.shape[0]
    block_rows = min(512, total_rows)
    key_span = block_rows + WINDOW - 1
    pad_keys = jnp.concatenate([jnp.zeros((WINDOW - 1, HEAD), jnp.float32), keys])
    pad_values = jnp.concatenate([jnp.zeros((WINDOW - 1, HEAD), jnp.float32), values])
    pad_ids = jnp.concatenate([jnp.full((WINDOW - 1,), -1, jnp.int32), segment_ids])
    scale = HEAD ** (-0.5)

    def one_block(block_index):
        first_row = (block_index * block_rows).astype(jnp.int32)
        query_block = lax.dynamic_slice_in_dim(query, first_row, block_rows, 0)
        key_block = lax.dynamic_slice_in_dim(pad_keys, first_row, key_span, 0)
        value_block = lax.dynamic_slice_in_dim(pad_values, first_row, key_span, 0)
        row_ids = lax.dynamic_slice_in_dim(segment_ids, first_row, block_rows, 0)
        col_ids = lax.dynamic_slice_in_dim(pad_ids, first_row, key_span, 0)
        scores = low_back(jnp.einsum('qhd,kd->hqk', query_block, key_block, precision=highest) * scale)
        distance = jnp.arange(block_rows, dtype=jnp.int32)[:, None] + (WINDOW - 1) - jnp.arange(key_span, dtype=jnp.int32)[None, :]
        allowed = (distance >= 0) & (distance < WINDOW) & (row_ids[:, None] == col_ids[None, :])
        scores = jnp.where(allowed[None], scores, NEGATIVE)
        top = lax.optimization_barrier(jnp.max(scores, axis=-1, keepdims=True))
        weights = jnp.exp(scores - top)
        probs = low(weights / lax.optimization_barrier(jnp.sum(weights, axis=-1, keepdims=True)))
        mixed = jnp.einsum('hqk,kd->qhd', probs, value_block, precision=highest)
        return mixed.reshape(block_rows, HEADS * HEAD)
    blocks = lax.map(jax.checkpoint(one_block), jnp.arange(total_rows // block_rows, dtype=jnp.int32))
    return blocks.reshape(total_rows, HEADS * HEAD)

def reference(tokens, segment_ids, positions, query_weight, key_weight, value_weight, out_weight, gate_weight, up_weight, down_weight, gain_in, gain_query, gain_key, gain_attn, gain_pre, gain_ffn, cotangent):
    highest = lax.Precision.HIGHEST
    half_size = HEAD // 2
    freqs = BASE ** (-(jnp.arange(half_size, dtype=jnp.float32) * 2.0 / HEAD))
    angles = positions.astype(jnp.float32)[:, None] * freqs[None, :]
    cosine = jnp.cos(angles)
    sine = jnp.sin(angles)
    total_rows = tokens.shape[0]

    def forward(inputs, query_mat, key_mat, value_mat, out_mat, gate_mat, up_mat, down_mat, scale_in, scale_query, scale_key, scale_attn, scale_pre, scale_ffn):
        normed = low(rms_unit(inputs) * scale_in)
        query_raw = low_back(jnp.dot(normed, query_mat, precision=highest)).reshape(total_rows, HEADS, HEAD)
        key_raw = low_back(jnp.dot(normed, key_mat, precision=highest))
        value_low = low(low_back(jnp.dot(normed, value_mat, precision=highest)))
        query = low(rotate(rms_unit(query_raw) * scale_query, cosine[:, None, :], sine[:, None, :]))
        keys = low(rotate(rms_unit(key_raw) * scale_key, cosine, sine))
        attended = low(low_back(band_attention(query, keys, value_low, segment_ids)))
        branch = low_back(jnp.dot(attended, out_mat, precision=highest))
        middle = inputs + rms_unit(branch) * scale_attn
        fed = low(rms_unit(middle) * scale_pre)
        gate = low_back(jnp.dot(fed, gate_mat, precision=highest))
        upward = low_back(jnp.dot(fed, up_mat, precision=highest))
        hidden = low(jax.nn.gelu(gate, approximate=True) * upward)
        down = low_back(jnp.dot(hidden, down_mat, precision=highest))
        return middle + rms_unit(down) * scale_ffn
    floats = tuple((item.astype(jnp.float32) for item in (tokens, query_weight, key_weight, value_weight, out_weight, gate_weight, up_weight, down_weight, gain_in, gain_query, gain_key, gain_attn, gain_pre, gain_ffn)))
    result, pullback = jax.vjp(forward, *floats)
    grads = pullback(cotangent.astype(jnp.float32))
    return (result.astype(jnp.bfloat16), grads[0], grads[1], grads[2], grads[3], grads[4], grads[5], grads[6], grads[7], grads[8], grads[9], grads[10], grads[11], grads[12], grads[13])
```

```python
import jax
import jax.numpy as jnp
from jax import lax
from jax.sharding import PartitionSpec as P

HEADS = 4
HEAD = 256
WINDOW = 512


EPS = 1e-06
BASE = 10000.0
NEGATIVE = -1e30


def passed_along(value, axis, steps):
    count = lax.axis_size(axis)
    leading, last = (max(0, -steps), min(count, count - steps))
    return lax.ppermute(value, axis, [(source, source + steps) for source in range(leading, last)])


def rms_parts(entries):
    inverse = lax.rsqrt(jnp.mean(entries * entries, axis=-1, keepdims=True) + EPS)
    return (entries * inverse, inverse)


def rms_back(normal, inverse, grad):
    return inverse * (grad - normal * jnp.mean(grad * normal, axis=-1, keepdims=True))


def rotate(entries, cosine, sine):
    half_size = entries.shape[-1] // 2
    first = entries[..., :half_size]
    second = entries[..., half_size:]
    return jnp.concatenate(
        [first * cosine - second * sine, second * cosine + first * sine], axis=-1
    )


def geglu(gate, upward):
    return jax.nn.gelu(gate, approximate=True) * upward


def bits_of(count):
    return [1 << k for k in range(count.bit_length() - 1)]


def swap(value, axis, bit):
    count = lax.axis_size(axis)
    return lax.ppermute(value, axis, [(i, i ^ bit) for i in range(count)])


def has_bit(axis, bit):
    return (lax.axis_index(axis) // bit) % 2


def join(mine, other, axis, bit, dim):
    upper = has_bit(axis, bit) == 1
    return jnp.where(
        upper, jnp.concatenate([other, mine], dim), jnp.concatenate([mine, other], dim)
    )


def gather_rows(shard):
    held = shard[None]
    for bit in reversed(bits_of(lax.axis_size("fsdp"))):
        held = join(held, swap(held, "fsdp", bit), "fsdp", bit, 0)
    return reorder(held, lax.axis_size("fsdp"))


def reorder(held, count):
    bits = count.bit_length() - 1
    rest = held.shape[1:]
    return (
        held.reshape((2,) * bits + rest)
        .transpose(tuple(reversed(range(bits))) + tuple(range(bits, bits + len(rest))))
        .reshape((count,) + rest)
    )


def gather_spread(shard, dim, first_low):
    parts = lax.axis_size("seq")
    size = shard.shape[dim] // parts
    held = lax.dynamic_slice_in_dim(shard, lax.axis_index("seq") * size, size, dim)
    piece = held.shape
    bits = bits_of(lax.axis_size("fsdp"))
    held = held[None]
    for bit in reversed(bits[1:]):
        held = join(held, swap(held, "fsdp", bit), "fsdp", bit, 0)
    held = held[None]
    seq_bits = bits_of(parts)
    order = seq_bits if first_low else seq_bits[::-1]
    for bit in order:
        held = join(held, swap(held, "seq", bit), "seq", bit, 0)
    held = held[None]
    held = join(held, swap(held, "fsdp", 1), "fsdp", 1, 0)
    ns, nz = len(seq_bits), len(bits) - 1
    held = held.reshape((2,) + (2,) * (ns + nz) + piece)
    seq_axes = [1 + i for i in range(ns)]
    if not first_low:
        seq_axes = seq_axes[::-1]
    z_axes = [1 + ns + i for i in range(nz)][::-1]
    row, col = 1 + ns + nz, 2 + ns + nz
    lead = z_axes + [0]
    axes = lead + (seq_axes + [row, col] if dim == 0 else [row] + seq_axes + [col])
    held = held.transpose(axes)
    return held.reshape(lax.axis_size("fsdp") * shard.shape[0], shard.shape[1])


def halve(value, axis, bit, dim):
    size = value.shape[dim] // 2
    mine = has_bit(axis, bit)
    away = lax.dynamic_slice_in_dim(value, (1 - mine) * size, size, dim)
    keep = lax.dynamic_slice_in_dim(value, mine * size, size, dim)
    came = swap(away, axis, bit)
    return (keep.astype(jnp.float32) + came.astype(jnp.float32)).astype(jnp.bfloat16)


def reduce_rows(grad, dim, first_low):
    count = lax.axis_size("fsdp")
    bits = bits_of(count)
    rest = grad.shape[1:]
    mine = has_bit("fsdp", 1)
    held = grad.reshape((count // 2, 2) + rest)
    away = lax.dynamic_index_in_dim(held, 1 - mine, 1, keepdims=False)
    keep = lax.dynamic_index_in_dim(held, mine, 1, keepdims=False)
    came = swap(away, "fsdp", 1)
    held = (keep.astype(jnp.float32) + came.astype(jnp.float32)).astype(jnp.bfloat16)
    seq_bits = bits_of(lax.axis_size("seq"))
    order = seq_bits if first_low else seq_bits[::-1]
    for bit in order:
        held = halve(held, "seq", bit, dim + 1)
    for bit in bits[:0:-1]:
        held = halve(held, "fsdp", bit, 0)
    held = held[0]
    for bit in order[::-1]:
        held = join(held, swap(held, "seq", bit), "seq", bit, dim)
    return held.astype(jnp.float32)


def band_mask(first_row, block_rows, positions):
    distance = (
        WINDOW
        + jnp.arange(block_rows, dtype=jnp.int32)[:, None]
        - jnp.arange(block_rows + WINDOW, dtype=jnp.int32)[None, :]
    )
    last = jnp.minimum(positions[first_row : first_row + block_rows], WINDOW - 1)
    return (distance >= 0) & (distance <= last[:, None])


def block_scores(query_block, key_block, allowed, scale):
    scores = (
        jnp.einsum("qhd,kd->hqk", query_block, key_block, preferred_element_type=jnp.float32)
        * scale
    )
    return jnp.where(allowed[None], scores, NEGATIVE)


def on_device(
    tokens,
    segment_ids,
    positions,
    query_weight,
    key_weight,
    value_weight,
    out_weight,
    gate_weight,
    up_weight,
    down_weight,
    gain_in,
    gain_query,
    gain_key,
    gain_attn,
    gain_pre,
    gain_ffn,
    cotangent,
):
    count = lax.axis_size("fsdp")
    gains = (gain_in, gain_query, gain_key, gain_attn, gain_pre, gain_ffn)
    sizes = [item.shape[0] for item in gains]
    first = jnp.concatenate([query_weight, key_weight, value_weight], axis=1)
    rows_in, width = first.shape
    packed = jnp.concatenate(gains)
    packed = jnp.pad(packed[None], ((0, 15), (0, width - packed.shape[0])))
    first_all = gather_rows(jnp.concatenate([first, packed], axis=0))
    qkv_full = first_all[:, :rows_in].reshape(count * rows_in, width)
    wide = HEADS * HEAD
    gains_all = first_all[:, rows_in].astype(jnp.float32)
    scales, at = [], 0
    for size in sizes:
        scales.append(gains_all[:, at : at + size].reshape(count * size))
        at += size
    scale_in, scale_query, scale_key, scale_attn, scale_pre, scale_ffn = scales
    out_full = gather_spread(out_weight, 0, True)
    gate_full = gather_spread(gate_weight, 1, True)
    up_full = gather_spread(up_weight, 1, False)
    down_full = gather_spread(down_weight, 0, False)
    row_count = tokens.shape[0]
    block_rows = min(512, row_count)
    key_span = block_rows + WINDOW
    block_count = row_count // block_rows
    scale = HEAD ** (-0.5)
    inputs = tokens.astype(jnp.float32)
    unit_in, inv_in = rms_parts(inputs)
    normed = (unit_in * scale_in).astype(jnp.bfloat16)
    raw = jnp.dot(normed, qkv_full, preferred_element_type=jnp.float32)
    query_raw = raw[:, :wide].reshape(row_count, HEADS, HEAD)
    key_raw = raw[:, wide : wide + HEAD]
    value_raw = raw[:, wide + HEAD :]
    half_size = HEAD // 2
    freqs = BASE ** (-(jnp.arange(half_size, dtype=jnp.float32) * 2.0 / HEAD))
    angles = positions.astype(jnp.float32)[:, None] * freqs[None, :]
    cosine = jnp.cos(angles)
    sine = jnp.sin(angles)
    unit_query, inv_query = rms_parts(query_raw)
    query_rot = rotate(unit_query * scale_query, cosine[:, None, :], sine[:, None, :]).astype(
        jnp.bfloat16
    )
    unit_key, inv_key = rms_parts(key_raw)
    key_rot = rotate(unit_key * scale_key, cosine, sine).astype(jnp.bfloat16)
    value_low = value_raw.astype(jnp.bfloat16)
    tail_start = row_count - WINDOW
    both = jnp.concatenate([key_rot, value_low], axis=1)
    tail = passed_along(both[tail_start:], ("seq", "fsdp"), 1)
    both_ext = jnp.concatenate([tail, both])
    keys_ext = both_ext[:, :HEAD]
    values_ext = both_ext[:, HEAD:]
    mixed_blocks = []
    log_sums = []
    for block_index in range(block_count):
        first_row = block_index * block_rows
        allowed = band_mask(first_row, block_rows, positions)
        scores = block_scores(
            query_rot[first_row : first_row + block_rows],
            keys_ext[first_row : first_row + key_span],
            allowed,
            scale,
        )
        top = jnp.max(scores, axis=-1, keepdims=True)
        weights = jnp.exp(scores - top)
        totals = jnp.sum(weights, axis=-1, keepdims=True)
        probs = (weights / totals).astype(jnp.bfloat16)
        mixed_blocks.append(
            jnp.einsum(
                "hqk,kd->qhd",
                probs,
                values_ext[first_row : first_row + key_span],
                preferred_element_type=jnp.float32,
            )
        )
        log_sums.append(top + jnp.log(totals))
    attended = jnp.concatenate(mixed_blocks).reshape(row_count, HEADS * HEAD).astype(jnp.bfloat16)
    branch = jnp.dot(attended, out_full, preferred_element_type=jnp.float32)
    unit_branch, inv_branch = rms_parts(branch)
    middle = inputs + unit_branch * scale_attn
    unit_mid, inv_mid = rms_parts(middle)
    fed = (unit_mid * scale_pre).astype(jnp.bfloat16)
    gate = jnp.dot(fed, gate_full, preferred_element_type=jnp.float32)
    upward = jnp.dot(fed, up_full, preferred_element_type=jnp.float32)
    geglu_value, geglu_pull = jax.vjp(geglu, gate, upward)
    hidden = geglu_value.astype(jnp.bfloat16)
    down = jnp.dot(hidden, down_full, preferred_element_type=jnp.float32)
    unit_down, inv_down = rms_parts(down)
    output = (middle + unit_down * scale_ffn).astype(jnp.bfloat16)
    upstream = cotangent.astype(jnp.float32)
    grad_scale_ffn = jnp.sum(upstream * unit_down, axis=0)
    d_down = rms_back(unit_down, inv_down, upstream * scale_ffn).astype(jnp.bfloat16)
    grad_down = jnp.einsum("tf,td->fd", hidden, d_down, preferred_element_type=jnp.float32)
    low_down = grad_down.astype(jnp.bfloat16).reshape(count, -1, grad_down.shape[1])
    low_down, d_down = lax.optimization_barrier((low_down, d_down))
    grad_down = reduce_rows(low_down, 0, True)
    d_hidden = jnp.einsum("td,fd->tf", d_down, down_full, preferred_element_type=jnp.float32)
    d_gate, d_up = geglu_pull(d_hidden)
    d_gate = d_gate.astype(jnp.bfloat16)
    d_up = d_up.astype(jnp.bfloat16)
    grad_gate = jnp.einsum("td,tf->df", fed, d_gate, preferred_element_type=jnp.float32)
    grad_up = jnp.einsum("td,tf->df", fed, d_up, preferred_element_type=jnp.float32)
    low_gate = grad_gate.astype(jnp.bfloat16).reshape(count, -1, grad_gate.shape[1])
    low_up = grad_up.astype(jnp.bfloat16).reshape(count, -1, grad_up.shape[1])
    low_gate, low_up, d_gate, d_up = lax.optimization_barrier((low_gate, low_up, d_gate, d_up))
    grad_gate = reduce_rows(low_gate, 1, True)
    grad_up = reduce_rows(low_up, 1, False)
    d_fed = jnp.einsum(
        "tf,df->td", d_gate, gate_full, preferred_element_type=jnp.float32
    ) + jnp.einsum("tf,df->td", d_up, up_full, preferred_element_type=jnp.float32)
    grad_scale_pre = jnp.sum(d_fed * unit_mid, axis=0)
    d_middle = upstream + rms_back(unit_mid, inv_mid, d_fed * scale_pre)
    grad_scale_attn = jnp.sum(d_middle * unit_branch, axis=0)
    d_branch = rms_back(unit_branch, inv_branch, d_middle * scale_attn).astype(jnp.bfloat16)
    grad_out = jnp.einsum("te,td->ed", attended, d_branch, preferred_element_type=jnp.float32)
    low_out = grad_out.astype(jnp.bfloat16).reshape(count, -1, grad_out.shape[1])
    low_out, d_branch = lax.optimization_barrier((low_out, d_branch))
    grad_out = reduce_rows(low_out, 0, False)
    d_attended = (
        jnp.einsum("td,ed->te", d_branch, out_full, preferred_element_type=jnp.float32)
        .astype(jnp.bfloat16)
        .reshape(row_count, HEADS, HEAD)
    )
    d_keys = jnp.zeros((row_count + WINDOW, HEAD), jnp.float32)
    d_values = jnp.zeros((row_count + WINDOW, HEAD), jnp.float32)
    query_grads = []
    for block_index in range(block_count):
        first_row = block_index * block_rows
        allowed = band_mask(first_row, block_rows, positions)
        query_block = query_rot[first_row : first_row + block_rows]
        key_block = keys_ext[first_row : first_row + key_span]
        value_block = values_ext[first_row : first_row + key_span]
        grad_block = d_attended[first_row : first_row + block_rows]
        scores = block_scores(query_block, key_block, allowed, scale)
        probs = jnp.where(allowed[None], jnp.exp(scores - log_sums[block_index]), 0.0)
        probs_low = probs.astype(jnp.bfloat16)
        d_values = d_values.at[first_row : first_row + key_span].add(
            jnp.einsum("hqk,qhd->kd", probs_low, grad_block, preferred_element_type=jnp.float32)
        )
        d_probs = jnp.einsum(
            "qhd,kd->hqk", grad_block, value_block, preferred_element_type=jnp.float32
        )
        centre = jnp.sum(probs * d_probs, axis=-1, keepdims=True)
        d_scores = (probs * (d_probs - centre)).astype(jnp.bfloat16)
        query_grads.append(
            jnp.einsum("hqk,kd->qhd", d_scores, key_block, preferred_element_type=jnp.float32)
            * scale
        )
        d_keys = d_keys.at[first_row : first_row + key_span].add(
            jnp.einsum("hqk,qhd->kd", d_scores, query_block, preferred_element_type=jnp.float32)
            * scale
        )
    back = passed_along(
        jnp.concatenate([d_keys[:WINDOW], d_values[:WINDOW]], axis=1).astype(jnp.bfloat16),
        ("seq", "fsdp"),
        -1,
    ).astype(jnp.float32)
    back = jnp.pad(back, ((tail_start, 0), (0, 0)))
    d_key = d_keys[WINDOW:] + back[:, :HEAD]
    d_value = d_values[WINDOW:] + back[:, HEAD:]
    d_query = jnp.concatenate(query_grads)
    turned_query = rotate(d_query, cosine[:, None, :], -sine[:, None, :])
    grad_scale_query = jnp.sum(turned_query * unit_query, axis=(0, 1))
    d_query_raw = (
        rms_back(unit_query, inv_query, turned_query * scale_query)
        .astype(jnp.bfloat16)
        .reshape(row_count, HEADS * HEAD)
    )
    turned_key = rotate(d_key, cosine, -sine)
    grad_scale_key = jnp.sum(turned_key * unit_key, axis=0)
    d_key_raw = rms_back(unit_key, inv_key, turned_key * scale_key).astype(jnp.bfloat16)
    d_value_raw = d_value.astype(jnp.bfloat16)
    d_raw = jnp.concatenate([d_query_raw, d_key_raw, d_value_raw], axis=1)
    grad_qkv = jnp.einsum("td,te->de", normed, d_raw, preferred_element_type=jnp.float32)
    low_qkv = grad_qkv.astype(jnp.bfloat16).reshape(count, rows_in, width)
    low_qkv, d_raw = lax.optimization_barrier((low_qkv, d_raw))
    grad_query = reduce_rows(low_qkv[:, :, :wide], 1, True)
    d_normed = jnp.einsum("te,de->td", d_raw, qkv_full, preferred_element_type=jnp.float32)
    grad_scale_in = jnp.sum(d_normed * unit_in, axis=0)
    grad_tokens = d_middle + rms_back(unit_in, inv_in, d_normed * scale_in)
    terms = [grad_scale_in, grad_scale_query, grad_scale_key]
    terms += [grad_scale_attn, grad_scale_pre, grad_scale_ffn]
    terms = jnp.concatenate([item.reshape(count, -1) for item in terms], axis=1)
    terms = jnp.pad(terms[:, None], ((0, 0), (0, 15), (0, 2 * HEAD - terms.shape[1])))
    rest = jnp.concatenate([low_qkv[:, :, wide:], terms.astype(jnp.bfloat16)], axis=1)
    rest = reduce_rows(rest, 1, False)
    grad_key = rest[:rows_in, :HEAD]
    grad_value = rest[:rows_in, HEAD:]
    gain_grads, at = [], 0
    for size in sizes:
        gain_grads.append(rest[rows_in, at : at + size])
        at += size
    return (
        output,
        grad_tokens,
        grad_query,
        grad_key,
        grad_value,
        grad_out,
        grad_gate,
        grad_up,
        grad_down,
        *gain_grads,
    )


def solution(mesh):
    in_specs = (
        P(("seq", "fsdp"), None),
        P(("seq", "fsdp")),
        P(("seq", "fsdp")),
        P("fsdp", None),
        P("fsdp", None),
        P("fsdp", None),
        P("fsdp", None),
        P("fsdp", None),
        P("fsdp", None),
        P("fsdp", None),
        P("fsdp"),
        P("fsdp"),
        P("fsdp"),
        P("fsdp"),
        P("fsdp"),
        P("fsdp"),
        P(("seq", "fsdp"), None),
    )
    out_specs = (
        P(("seq", "fsdp"), None),
        P(("seq", "fsdp"), None),
        P("fsdp", None),
        P("fsdp", None),
        P("fsdp", None),
        P("fsdp", None),
        P("fsdp", None),
        P("fsdp", None),
        P("fsdp", None),
        P("fsdp"),
        P("fsdp"),
        P("fsdp"),
        P("fsdp"),
        P("fsdp"),
        P("fsdp"),
    )
    return jax.shard_map(
        on_device, mesh=mesh, in_specs=in_specs, out_specs=out_specs, check_vma=False
    )
```

```python
import jax
import jax.numpy as jnp
from jax import lax
from jax.sharding import PartitionSpec as P

HEADS = 4
HEAD = 256
WINDOW = 512


EPS = 1e-06
BASE = 10000.0
NEGATIVE = -1e30


def passed_along(value, axis, steps):
    count = lax.axis_size(axis)
    leading, last = (max(0, -steps), min(count, count - steps))
    return lax.ppermute(value, axis, [(source, source + steps) for source in range(leading, last)])


def rms_parts(entries):
    inverse = lax.rsqrt(jnp.mean(entries * entries, axis=-1, keepdims=True) + EPS)
    return (entries * inverse, inverse)


def rms_back(normal, inverse, grad):
    return inverse * (grad - normal * jnp.mean(grad * normal, axis=-1, keepdims=True))


def rotate(entries, cosine, sine):
    half_size = entries.shape[-1] // 2
    first = entries[..., :half_size]
    second = entries[..., half_size:]
    return jnp.concatenate(
        [first * cosine - second * sine, second * cosine + first * sine], axis=-1
    )


def geglu(gate, upward):
    return jax.nn.gelu(gate, approximate=True) * upward


def bits_of(count):
    return [1 << k for k in range(count.bit_length() - 1)]


def swap(value, axis, bit):
    count = lax.axis_size(axis)
    return lax.ppermute(value, axis, [(i, i ^ bit) for i in range(count)])


def has_bit(axis, bit):
    return (lax.axis_index(axis) // bit) % 2


def join(mine, other, axis, bit, dim):
    upper = has_bit(axis, bit) == 1
    return jnp.where(
        upper, jnp.concatenate([other, mine], dim), jnp.concatenate([mine, other], dim)
    )


def stack_bit(held, bit, place):
    mine = jnp.expand_dims(held, place)
    return join(mine, jnp.expand_dims(swap(held, "fsdp", bit), place), "fsdp", bit, place)


def gather_rows(shard):
    count = lax.axis_size("fsdp")
    held = shard
    for place, bit in enumerate(reversed(bits_of(count))):
        held = stack_bit(held, bit, place)
    return held.reshape((count,) + shard.shape)


class Stages:
    def __init__(self, held, steps):
        self.held = held
        self.steps = steps

    def step(self):
        self.held = self.steps.pop(0)(self.held)

    def finish(self):
        while self.steps:
            self.step()
        return self.held


def advance(groups, *values):
    active = [group for group in groups if group.steps]
    for group in active:
        group.step()
    helds, values = lax.optimization_barrier(([group.held for group in active], values))
    for group, held in zip(active, helds):
        group.held = held
    return values if len(values) > 1 else values[0]


def seq_order(low_first):
    bits = bits_of(lax.axis_size("seq"))
    return bits if low_first else bits[::-1]


def gather_spread(shard, dim, low_first):
    count = lax.axis_size("fsdp")
    size = shard.shape[dim] // lax.axis_size("seq")
    order = seq_order(low_first)
    part = sum(has_bit("seq", bit) * (1 << k) for k, bit in enumerate(order))
    bits = bits_of(count)
    lead = len(bits) - 1

    def fetch(bit, place):
        return lambda held: stack_bit(held, bit, place)

    def share(bit):
        return lambda held: join(held, swap(held, "seq", bit), "seq", bit, lead + dim)

    steps = [fetch(bit, place) for place, bit in enumerate(bits[:0:-1])]
    steps += [share(bit) for bit in order]
    steps += [fetch(1, lead)]
    return Stages(lax.dynamic_slice_in_dim(shard, part * size, size, dim), steps)


def halve(value, axis, bit, dim):
    size = value.shape[dim] // 2
    mine = has_bit(axis, bit)
    away = lax.dynamic_slice_in_dim(value, (1 - mine) * size, size, dim)
    keep = lax.dynamic_slice_in_dim(value, mine * size, size, dim)
    came = swap(away, axis, bit)
    return (keep.astype(jnp.float32) + came.astype(jnp.float32)).astype(jnp.bfloat16)


def reduce_rows(grad, dim, low_first):
    count = lax.axis_size("fsdp")
    bits = bits_of(count)
    rest = grad.shape[1:]
    order = seq_order(low_first)

    def pair(held):
        mine = has_bit("fsdp", 1)
        away = lax.dynamic_index_in_dim(held, 1 - mine, 1, keepdims=False)
        keep = lax.dynamic_index_in_dim(held, mine, 1, keepdims=False)
        came = swap(away, "fsdp", 1)
        return (keep.astype(jnp.float32) + came.astype(jnp.float32)).astype(jnp.bfloat16)

    def cut(axis, bit, place):
        return lambda held: halve(held, axis, bit, place)

    def share(bit):
        return lambda held: join(held, swap(held, "seq", bit), "seq", bit, dim + 1)

    steps = [pair] + [cut("seq", bit, dim + 1) for bit in order]
    steps += [cut("fsdp", bit, 0) for bit in bits[:0:-1]]
    steps += [share(bit) for bit in order[::-1]]
    return Stages(grad.reshape((count // 2, 2) + rest), steps)


def band_mask(first_row, block_rows, positions):
    distance = (
        WINDOW
        + jnp.arange(block_rows, dtype=jnp.int32)[:, None]
        - jnp.arange(block_rows + WINDOW, dtype=jnp.int32)[None, :]
    )
    last = jnp.minimum(positions[first_row : first_row + block_rows], WINDOW - 1)
    return (distance >= 0) & (distance <= last[:, None])


def block_scores(query_block, key_block, allowed, scale):
    scores = (
        jnp.einsum("qhd,kd->hqk", query_block, key_block, preferred_element_type=jnp.float32)
        * scale
    )
    return jnp.where(allowed[None], scores, NEGATIVE)


def on_device(
    tokens,
    segment_ids,
    positions,
    query_weight,
    key_weight,
    value_weight,
    out_weight,
    gate_weight,
    up_weight,
    down_weight,
    gain_in,
    gain_query,
    gain_key,
    gain_attn,
    gain_pre,
    gain_ffn,
    cotangent,
):
    count = lax.axis_size("fsdp")
    gains = (gain_in, gain_query, gain_key, gain_attn, gain_pre, gain_ffn)
    sizes = [item.shape[0] for item in gains]
    first = jnp.concatenate([query_weight, key_weight, value_weight], axis=1)
    rows_in, width = first.shape
    packed = jnp.concatenate(gains)
    packed = jnp.pad(packed[None], ((0, 15), (0, width - packed.shape[0])))
    first_all = gather_rows(jnp.concatenate([first, packed], axis=0))
    qkv_full = first_all[:, :rows_in].reshape(count * rows_in, width)
    wide = HEADS * HEAD
    gains_all = first_all[:, rows_in].astype(jnp.float32)
    scales, at = [], 0
    for size in sizes:
        scales.append(gains_all[:, at : at + size].reshape(count * size))
        at += size
    scale_in, scale_query, scale_key, scale_attn, scale_pre, scale_ffn = scales
    qkv_full, later = lax.optimization_barrier(
        (qkv_full, (out_weight, gate_weight, up_weight, down_weight))
    )
    groups = [
        gather_spread(later[0], 0, True),
        gather_spread(later[1], 1, True),
        gather_spread(later[2], 1, False),
        gather_spread(later[3], 0, False),
    ]
    row_count = tokens.shape[0]
    block_rows = min(512, row_count)
    key_span = block_rows + WINDOW
    block_count = row_count // block_rows
    scale = HEAD ** (-0.5)
    inputs = tokens.astype(jnp.float32)
    unit_in, inv_in = rms_parts(inputs)
    normed = (unit_in * scale_in).astype(jnp.bfloat16)
    raw = jnp.dot(normed, qkv_full, preferred_element_type=jnp.float32)
    raw = advance(groups, raw)
    query_raw = raw[:, :wide].reshape(row_count, HEADS, HEAD)
    key_raw = raw[:, wide : wide + HEAD]
    value_raw = raw[:, wide + HEAD :]
    half_size = HEAD // 2
    freqs = BASE ** (-(jnp.arange(half_size, dtype=jnp.float32) * 2.0 / HEAD))
    angles = positions.astype(jnp.float32)[:, None] * freqs[None, :]
    cosine = jnp.cos(angles)
    sine = jnp.sin(angles)
    unit_query, inv_query = rms_parts(query_raw)
    query_rot = rotate(unit_query * scale_query, cosine[:, None, :], sine[:, None, :]).astype(
        jnp.bfloat16
    )
    unit_key, inv_key = rms_parts(key_raw)
    key_rot = rotate(unit_key * scale_key, cosine, sine).astype(jnp.bfloat16)
    value_low = value_raw.astype(jnp.bfloat16)
    query_rot, key_rot = advance(groups, query_rot, key_rot)
    tail_start = row_count - WINDOW
    both = jnp.concatenate([key_rot, value_low], axis=1)
    tail = passed_along(both[tail_start:], ("seq", "fsdp"), 1)
    both_ext = jnp.concatenate([tail, both])
    keys_ext = both_ext[:, :HEAD]
    values_ext = both_ext[:, HEAD:]
    mixed_blocks = []
    log_sums = []
    for block_index in range(block_count):
        first_row = block_index * block_rows
        allowed = band_mask(first_row, block_rows, positions)
        scores = block_scores(
            query_rot[first_row : first_row + block_rows],
            keys_ext[first_row : first_row + key_span],
            allowed,
            scale,
        )
        scores = advance(groups, scores)
        top = jnp.max(scores, axis=-1, keepdims=True)
        weights = jnp.exp(scores - top)
        totals = jnp.sum(weights, axis=-1, keepdims=True)
        probs = (weights / totals).astype(jnp.bfloat16)
        mixed_blocks.append(
            jnp.einsum(
                "hqk,kd->qhd",
                probs,
                values_ext[first_row : first_row + key_span],
                preferred_element_type=jnp.float32,
            )
        )
        mixed_blocks[-1] = advance(groups, mixed_blocks[-1])
        log_sums.append(top + jnp.log(totals))
    attended = jnp.concatenate(mixed_blocks).reshape(row_count, HEADS * HEAD).astype(jnp.bfloat16)
    out_full, gate_full, up_full, down_full = [
        group.finish().reshape(count * shard.shape[0], shard.shape[1])
        for group, shard in zip(groups, (out_weight, gate_weight, up_weight, down_weight))
    ]
    branch = jnp.dot(attended, out_full, preferred_element_type=jnp.float32)
    unit_branch, inv_branch = rms_parts(branch)
    middle = inputs + unit_branch * scale_attn
    unit_mid, inv_mid = rms_parts(middle)
    fed = (unit_mid * scale_pre).astype(jnp.bfloat16)
    gate = jnp.dot(fed, gate_full, preferred_element_type=jnp.float32)
    upward = jnp.dot(fed, up_full, preferred_element_type=jnp.float32)
    geglu_value, geglu_pull = jax.vjp(geglu, gate, upward)
    hidden = geglu_value.astype(jnp.bfloat16)
    down = jnp.dot(hidden, down_full, preferred_element_type=jnp.float32)
    unit_down, inv_down = rms_parts(down)
    output = (middle + unit_down * scale_ffn).astype(jnp.bfloat16)
    upstream = cotangent.astype(jnp.float32)
    grad_scale_ffn = jnp.sum(upstream * unit_down, axis=0)
    d_down = rms_back(unit_down, inv_down, upstream * scale_ffn).astype(jnp.bfloat16)
    grad_down = jnp.einsum("tf,td->fd", hidden, d_down, preferred_element_type=jnp.float32)
    low_down = grad_down.astype(jnp.bfloat16).reshape(count, -1, grad_down.shape[1])
    low_down, d_down = lax.optimization_barrier((low_down, d_down))
    sum_down = reduce_rows(low_down, 0, True)
    sums = [sum_down]
    d_hidden = jnp.einsum("td,fd->tf", d_down, down_full, preferred_element_type=jnp.float32)
    d_gate, d_up = geglu_pull(d_hidden)
    d_gate = d_gate.astype(jnp.bfloat16)
    d_up = d_up.astype(jnp.bfloat16)
    d_gate, d_up = advance(sums, d_gate, d_up)
    grad_gate = jnp.einsum("td,tf->df", fed, d_gate, preferred_element_type=jnp.float32)
    grad_up = jnp.einsum("td,tf->df", fed, d_up, preferred_element_type=jnp.float32)
    low_gate = grad_gate.astype(jnp.bfloat16).reshape(count, -1, grad_gate.shape[1])
    low_up = grad_up.astype(jnp.bfloat16).reshape(count, -1, grad_up.shape[1])
    low_gate, low_up, d_gate, d_up = advance(sums, low_gate, low_up, d_gate, d_up)
    sum_gate = reduce_rows(low_gate, 1, True)
    sum_up = reduce_rows(low_up, 1, False)
    sums += [sum_gate, sum_up]
    d_fed = jnp.einsum(
        "tf,df->td", d_gate, gate_full, preferred_element_type=jnp.float32
    ) + jnp.einsum("tf,df->td", d_up, up_full, preferred_element_type=jnp.float32)
    grad_scale_pre = jnp.sum(d_fed * unit_mid, axis=0)
    d_middle = upstream + rms_back(unit_mid, inv_mid, d_fed * scale_pre)
    grad_scale_attn = jnp.sum(d_middle * unit_branch, axis=0)
    d_branch = rms_back(unit_branch, inv_branch, d_middle * scale_attn).astype(jnp.bfloat16)
    grad_out = jnp.einsum("te,td->ed", attended, d_branch, preferred_element_type=jnp.float32)
    low_out = grad_out.astype(jnp.bfloat16).reshape(count, -1, grad_out.shape[1])
    low_out, d_branch = advance(sums, low_out, d_branch)
    sum_out = reduce_rows(low_out, 0, False)
    sums += [sum_out]
    d_attended = (
        jnp.einsum("td,ed->te", d_branch, out_full, preferred_element_type=jnp.float32)
        .astype(jnp.bfloat16)
        .reshape(row_count, HEADS, HEAD)
    )
    d_keys = jnp.zeros((row_count + WINDOW, HEAD), jnp.float32)
    d_values = jnp.zeros((row_count + WINDOW, HEAD), jnp.float32)
    query_grads = []
    for block_index in range(block_count):
        first_row = block_index * block_rows
        allowed = band_mask(first_row, block_rows, positions)
        query_block = query_rot[first_row : first_row + block_rows]
        key_block = keys_ext[first_row : first_row + key_span]
        value_block = values_ext[first_row : first_row + key_span]
        grad_block = d_attended[first_row : first_row + block_rows]
        scores = block_scores(query_block, key_block, allowed, scale)
        probs = jnp.where(allowed[None], jnp.exp(scores - log_sums[block_index]), 0.0)
        probs_low = probs.astype(jnp.bfloat16)
        d_values = d_values.at[first_row : first_row + key_span].add(
            jnp.einsum("hqk,qhd->kd", probs_low, grad_block, preferred_element_type=jnp.float32)
        )
        d_probs = jnp.einsum(
            "qhd,kd->hqk", grad_block, value_block, preferred_element_type=jnp.float32
        )
        d_probs = advance(sums, d_probs)
        centre = jnp.sum(probs * d_probs, axis=-1, keepdims=True)
        d_scores = (probs * (d_probs - centre)).astype(jnp.bfloat16)
        d_scores = advance(sums, d_scores)
        query_grads.append(
            jnp.einsum("hqk,kd->qhd", d_scores, key_block, preferred_element_type=jnp.float32)
            * scale
        )
        d_keys = d_keys.at[first_row : first_row + key_span].add(
            jnp.einsum("hqk,qhd->kd", d_scores, query_block, preferred_element_type=jnp.float32)
            * scale
        )
    back = passed_along(
        jnp.concatenate([d_keys[:WINDOW], d_values[:WINDOW]], axis=1).astype(jnp.bfloat16),
        ("seq", "fsdp"),
        -1,
    ).astype(jnp.float32)
    back = jnp.pad(back, ((tail_start, 0), (0, 0)))
    d_key = d_keys[WINDOW:] + back[:, :HEAD]
    d_value = d_values[WINDOW:] + back[:, HEAD:]
    d_query = jnp.concatenate(query_grads)
    turned_query = rotate(d_query, cosine[:, None, :], -sine[:, None, :])
    grad_scale_query = jnp.sum(turned_query * unit_query, axis=(0, 1))
    d_query_raw = (
        rms_back(unit_query, inv_query, turned_query * scale_query)
        .astype(jnp.bfloat16)
        .reshape(row_count, HEADS * HEAD)
    )
    turned_key = rotate(d_key, cosine, -sine)
    grad_scale_key = jnp.sum(turned_key * unit_key, axis=0)
    d_key_raw = rms_back(unit_key, inv_key, turned_key * scale_key).astype(jnp.bfloat16)
    d_value_raw = d_value.astype(jnp.bfloat16)
    d_query_raw = advance(sums, d_query_raw)
    d_raw = jnp.concatenate([d_query_raw, d_key_raw, d_value_raw], axis=1)
    grad_qkv = jnp.einsum("td,te->de", normed, d_raw, preferred_element_type=jnp.float32)
    low_qkv = grad_qkv.astype(jnp.bfloat16).reshape(count, rows_in, width)
    low_qkv, d_raw = advance(sums, low_qkv, d_raw)
    sum_query = reduce_rows(low_qkv[:, :, :wide], 1, True)
    d_normed = jnp.einsum("te,de->td", d_raw, qkv_full, preferred_element_type=jnp.float32)
    grad_scale_in = jnp.sum(d_normed * unit_in, axis=0)
    grad_tokens = d_middle + rms_back(unit_in, inv_in, d_normed * scale_in)
    terms = [grad_scale_in, grad_scale_query, grad_scale_key]
    terms += [grad_scale_attn, grad_scale_pre, grad_scale_ffn]
    terms = jnp.concatenate([item.reshape(count, -1) for item in terms], axis=1)
    terms = jnp.pad(terms[:, None], ((0, 0), (0, 15), (0, 2 * HEAD - terms.shape[1])))
    rest = jnp.concatenate([low_qkv[:, :, wide:], terms.astype(jnp.bfloat16)], axis=1)
    sum_rest = reduce_rows(rest, 1, False)
    sums += [sum_query, sum_rest]
    ends = [group.finish()[0].astype(jnp.float32) for group in sums]
    grad_down, grad_gate, grad_up, grad_out, grad_query, rest = ends
    grad_key = rest[:rows_in, :HEAD]
    grad_value = rest[:rows_in, HEAD:]
    gain_grads, at = [], 0
    for size in sizes:
        gain_grads.append(rest[rows_in, at : at + size])
        at += size
    return (
        output,
        grad_tokens,
        grad_query,
        grad_key,
        grad_value,
        grad_out,
        grad_gate,
        grad_up,
        grad_down,
        *gain_grads,
    )


def solution(mesh):
    in_specs = (
        P(("seq", "fsdp"), None),
        P(("seq", "fsdp")),
        P(("seq", "fsdp")),
        P("fsdp", None),
        P("fsdp", None),
        P("fsdp", None),
        P("fsdp", None),
        P("fsdp", None),
        P("fsdp", None),
        P("fsdp", None),
        P("fsdp"),
        P("fsdp"),
        P("fsdp"),
        P("fsdp"),
        P("fsdp"),
        P("fsdp"),
        P(("seq", "fsdp"), None),
    )
    out_specs = (
        P(("seq", "fsdp"), None),
        P(("seq", "fsdp"), None),
        P("fsdp", None),
        P("fsdp", None),
        P("fsdp", None),
        P("fsdp", None),
        P("fsdp", None),
        P("fsdp", None),
        P("fsdp", None),
        P("fsdp"),
        P("fsdp"),
        P("fsdp"),
        P("fsdp"),
        P("fsdp"),
        P("fsdp"),
    )
    return jax.shard_map(
        on_device, mesh=mesh, in_specs=in_specs, out_specs=out_specs, check_vma=False
    )
```

```python
import jax
import jax.numpy as jnp
from jax import lax
from jax.sharding import PartitionSpec as P

HEADS = 4
HEAD = 256
WINDOW = 512


EPS = 1e-06
BASE = 10000.0
NEGATIVE = -1e30


def passed_along(value, axis, steps):
    count = lax.axis_size(axis)
    leading, last = (max(0, -steps), min(count, count - steps))
    return lax.ppermute(value, axis, [(source, source + steps) for source in range(leading, last)])


def rms_parts(entries):
    inverse = lax.rsqrt(jnp.mean(entries * entries, axis=-1, keepdims=True) + EPS)
    return (entries * inverse, inverse)


def rms_back(normal, inverse, grad):
    return inverse * (grad - normal * jnp.mean(grad * normal, axis=-1, keepdims=True))


def rotate(entries, cosine, sine):
    half_size = entries.shape[-1] // 2
    first = entries[..., :half_size]
    second = entries[..., half_size:]
    return jnp.concatenate(
        [first * cosine - second * sine, second * cosine + first * sine], axis=-1
    )


def geglu(gate, upward):
    return jax.nn.gelu(gate, approximate=True) * upward


def bits_of(count):
    return [1 << k for k in range(count.bit_length() - 1)]


def swap(value, axis, bit):
    count = lax.axis_size(axis)
    return lax.ppermute(value, axis, [(i, i ^ bit) for i in range(count)])


def has_bit(axis, bit):
    return (lax.axis_index(axis) // bit) % 2


def join(mine, other, axis, bit, dim):
    upper = has_bit(axis, bit) == 1
    return jnp.where(
        upper, jnp.concatenate([other, mine], dim), jnp.concatenate([mine, other], dim)
    )


def stack_bit(held, bit, place):
    mine = jnp.expand_dims(held, place)
    return join(mine, jnp.expand_dims(swap(held, "fsdp", bit), place), "fsdp", bit, place)


def gather_rows(shard):
    count = lax.axis_size("fsdp")
    held = shard
    for place, bit in enumerate(reversed(bits_of(count))):
        held = stack_bit(held, bit, place)
    return held.reshape((count,) + shard.shape)


class Stages:
    def __init__(self, held, steps):
        self.held = held
        self.steps = steps

    def step(self):
        self.held = self.steps.pop(0)(self.held)

    def finish(self):
        while self.steps:
            self.step()
        return self.held


def advance(groups, *values, times=1):
    active = [group for group in groups if group.steps]
    for group in active:
        for _ in range(min(times, len(group.steps))):
            group.step()
    helds, values = lax.optimization_barrier(([group.held for group in active], values))
    for group, held in zip(active, helds):
        group.held = held
    return values if len(values) > 1 else values[0]


def seq_order(low_first):
    bits = bits_of(lax.axis_size("seq"))
    return bits if low_first else bits[::-1]


def gather_spread(shard, dim, low_first):
    count = lax.axis_size("fsdp")
    size = shard.shape[dim] // lax.axis_size("seq")
    order = seq_order(low_first)
    part = sum(has_bit("seq", bit) * (1 << k) for k, bit in enumerate(order))
    bits = bits_of(count)
    lead = len(bits) - 1

    def fetch(bit, place):
        return lambda held: stack_bit(held, bit, place)

    def share(bit):
        return lambda held: join(held, swap(held, "seq", bit), "seq", bit, lead + dim)

    steps = [fetch(bit, place) for place, bit in enumerate(bits[:0:-1])]
    steps += [share(bit) for bit in order]
    steps += [fetch(1, lead)]
    return Stages(lax.dynamic_slice_in_dim(shard, part * size, size, dim), steps)


def halve(value, axis, bit, dim):
    size = value.shape[dim] // 2
    mine = has_bit(axis, bit)
    away = lax.dynamic_slice_in_dim(value, (1 - mine) * size, size, dim)
    keep = lax.dynamic_slice_in_dim(value, mine * size, size, dim)
    came = swap(away, axis, bit)
    return (keep.astype(jnp.float32) + came.astype(jnp.float32)).astype(jnp.bfloat16)


def reduce_rows(grad, dim, low_first):
    count = lax.axis_size("fsdp")
    bits = bits_of(count)
    rest = grad.shape[1:]
    order = seq_order(low_first)

    def pair(held):
        mine = has_bit("fsdp", 1)
        away = lax.dynamic_index_in_dim(held, 1 - mine, 1, keepdims=False)
        keep = lax.dynamic_index_in_dim(held, mine, 1, keepdims=False)
        came = swap(away, "fsdp", 1)
        return (keep.astype(jnp.float32) + came.astype(jnp.float32)).astype(jnp.bfloat16)

    def cut(axis, bit, place):
        return lambda held: halve(held, axis, bit, place)

    def share(bit):
        return lambda held: join(held, swap(held, "seq", bit), "seq", bit, dim + 1)

    steps = [pair] + [cut("seq", bit, dim + 1) for bit in order]
    steps += [cut("fsdp", bit, 0) for bit in bits[:0:-1]]
    steps += [share(bit) for bit in order[::-1]]
    return Stages(grad.reshape((count // 2, 2) + rest), steps)


def band_mask(first_row, block_rows, positions):
    distance = (
        WINDOW
        + jnp.arange(block_rows, dtype=jnp.int32)[:, None]
        - jnp.arange(block_rows + WINDOW, dtype=jnp.int32)[None, :]
    )
    last = jnp.minimum(positions[first_row : first_row + block_rows], WINDOW - 1)
    return (distance >= 0) & (distance <= last[:, None])


def block_scores(query_block, key_block, allowed, scale):
    scores = (
        jnp.einsum("qhd,kd->hqk", query_block, key_block, preferred_element_type=jnp.float32)
        * scale
    )
    return jnp.where(allowed[None], scores, NEGATIVE)


def on_device(
    tokens,
    segment_ids,
    positions,
    query_weight,
    key_weight,
    value_weight,
    out_weight,
    gate_weight,
    up_weight,
    down_weight,
    gain_in,
    gain_query,
    gain_key,
    gain_attn,
    gain_pre,
    gain_ffn,
    cotangent,
):
    count = lax.axis_size("fsdp")
    gains = (gain_in, gain_query, gain_key, gain_attn, gain_pre, gain_ffn)
    sizes = [item.shape[0] for item in gains]
    first = jnp.concatenate([query_weight, key_weight, value_weight], axis=1)
    rows_in, width = first.shape
    packed = jnp.concatenate(gains)
    packed = jnp.pad(packed[None], ((0, 15), (0, width - packed.shape[0])))
    first_all = gather_rows(jnp.concatenate([first, packed], axis=0))
    qkv_full = first_all[:, :rows_in].reshape(count * rows_in, width)
    wide = HEADS * HEAD
    gains_all = first_all[:, rows_in].astype(jnp.float32)
    scales, at = [], 0
    for size in sizes:
        scales.append(gains_all[:, at : at + size].reshape(count * size))
        at += size
    scale_in, scale_query, scale_key, scale_attn, scale_pre, scale_ffn = scales
    qkv_full, later = lax.optimization_barrier(
        (qkv_full, (out_weight, gate_weight, up_weight, down_weight))
    )
    groups = [
        gather_spread(later[0], 0, True),
        gather_spread(later[1], 1, True),
        gather_spread(later[2], 1, False),
        gather_spread(later[3], 0, False),
    ]
    row_count = tokens.shape[0]
    block_rows = min(512, row_count)
    key_span = block_rows + WINDOW
    block_count = row_count // block_rows
    scale = HEAD ** (-0.5)
    inputs = tokens.astype(jnp.float32)
    unit_in, inv_in = rms_parts(inputs)
    normed = (unit_in * scale_in).astype(jnp.bfloat16)
    raw = jnp.dot(normed, qkv_full, preferred_element_type=jnp.float32)
    raw = advance(groups, raw)
    query_raw = raw[:, :wide].reshape(row_count, HEADS, HEAD)
    key_raw = raw[:, wide : wide + HEAD]
    value_raw = raw[:, wide + HEAD :]
    half_size = HEAD // 2
    freqs = BASE ** (-(jnp.arange(half_size, dtype=jnp.float32) * 2.0 / HEAD))
    angles = positions.astype(jnp.float32)[:, None] * freqs[None, :]
    cosine = jnp.cos(angles)
    sine = jnp.sin(angles)
    unit_query, inv_query = rms_parts(query_raw)
    query_rot = rotate(unit_query * scale_query, cosine[:, None, :], sine[:, None, :]).astype(
        jnp.bfloat16
    )
    unit_key, inv_key = rms_parts(key_raw)
    key_rot = rotate(unit_key * scale_key, cosine, sine).astype(jnp.bfloat16)
    value_low = value_raw.astype(jnp.bfloat16)
    query_rot, key_rot = advance(groups, query_rot, key_rot)
    tail_start = row_count - WINDOW
    both = jnp.concatenate([key_rot, value_low], axis=1)
    tail = passed_along(both[tail_start:], ("seq", "fsdp"), 1)
    both_ext = jnp.concatenate([tail, both])
    keys_ext = both_ext[:, :HEAD]
    values_ext = both_ext[:, HEAD:]
    mixed_blocks = []
    log_sums = []
    for block_index in range(block_count):
        first_row = block_index * block_rows
        allowed = band_mask(first_row, block_rows, positions)
        scores = block_scores(
            query_rot[first_row : first_row + block_rows],
            keys_ext[first_row : first_row + key_span],
            allowed,
            scale,
        )
        top = jnp.max(scores, axis=-1, keepdims=True)
        weights = jnp.exp(scores - top)
        totals = jnp.sum(weights, axis=-1, keepdims=True)
        probs = (weights / totals).astype(jnp.bfloat16)
        mixed_blocks.append(
            jnp.einsum(
                "hqk,kd->qhd",
                probs,
                values_ext[first_row : first_row + key_span],
                preferred_element_type=jnp.float32,
            )
        )
        mixed_blocks[-1] = advance(groups, mixed_blocks[-1])
        log_sums.append(top + jnp.log(totals))
    attended = jnp.concatenate(mixed_blocks).reshape(row_count, HEADS * HEAD).astype(jnp.bfloat16)
    out_full, gate_full, up_full, down_full = [
        group.finish().reshape(count * shard.shape[0], shard.shape[1])
        for group, shard in zip(groups, (out_weight, gate_weight, up_weight, down_weight))
    ]
    branch = jnp.dot(attended, out_full, preferred_element_type=jnp.float32)
    unit_branch, inv_branch = rms_parts(branch)
    middle = inputs + unit_branch * scale_attn
    unit_mid, inv_mid = rms_parts(middle)
    fed = (unit_mid * scale_pre).astype(jnp.bfloat16)
    gate = jnp.dot(fed, gate_full, preferred_element_type=jnp.float32)
    upward = jnp.dot(fed, up_full, preferred_element_type=jnp.float32)
    geglu_value, geglu_pull = jax.vjp(geglu, gate, upward)
    hidden = geglu_value.astype(jnp.bfloat16)
    down = jnp.dot(hidden, down_full, preferred_element_type=jnp.float32)
    unit_down, inv_down = rms_parts(down)
    output = (middle + unit_down * scale_ffn).astype(jnp.bfloat16)
    upstream = cotangent.astype(jnp.float32)
    grad_scale_ffn = jnp.sum(upstream * unit_down, axis=0)
    d_down = rms_back(unit_down, inv_down, upstream * scale_ffn).astype(jnp.bfloat16)
    grad_down = jnp.einsum("tf,td->fd", hidden, d_down, preferred_element_type=jnp.float32)
    low_down = grad_down.astype(jnp.bfloat16).reshape(count, -1, grad_down.shape[1])
    low_down, d_down = lax.optimization_barrier((low_down, d_down))
    sum_down = reduce_rows(low_down, 0, True)
    sums = [sum_down]
    d_hidden = jnp.einsum("td,fd->tf", d_down, down_full, preferred_element_type=jnp.float32)
    d_gate, d_up = geglu_pull(d_hidden)
    d_gate = d_gate.astype(jnp.bfloat16)
    d_up = d_up.astype(jnp.bfloat16)
    d_gate, d_up = advance(sums, d_gate, d_up)
    grad_gate = jnp.einsum("td,tf->df", fed, d_gate, preferred_element_type=jnp.float32)
    grad_up = jnp.einsum("td,tf->df", fed, d_up, preferred_element_type=jnp.float32)
    low_gate = grad_gate.astype(jnp.bfloat16).reshape(count, -1, grad_gate.shape[1])
    low_up = grad_up.astype(jnp.bfloat16).reshape(count, -1, grad_up.shape[1])
    low_gate, low_up, d_gate, d_up = advance(sums, low_gate, low_up, d_gate, d_up)
    sum_gate = reduce_rows(low_gate, 1, True)
    sum_up = reduce_rows(low_up, 1, False)
    sums += [sum_gate, sum_up]
    d_fed = jnp.einsum(
        "tf,df->td", d_gate, gate_full, preferred_element_type=jnp.float32
    ) + jnp.einsum("tf,df->td", d_up, up_full, preferred_element_type=jnp.float32)
    grad_scale_pre = jnp.sum(d_fed * unit_mid, axis=0)
    d_middle = upstream + rms_back(unit_mid, inv_mid, d_fed * scale_pre)
    grad_scale_attn = jnp.sum(d_middle * unit_branch, axis=0)
    d_branch = rms_back(unit_branch, inv_branch, d_middle * scale_attn).astype(jnp.bfloat16)
    grad_out = jnp.einsum("te,td->ed", attended, d_branch, preferred_element_type=jnp.float32)
    low_out = grad_out.astype(jnp.bfloat16).reshape(count, -1, grad_out.shape[1])
    low_out, d_branch = advance(sums, low_out, d_branch)
    sum_out = reduce_rows(low_out, 0, False)
    sums += [sum_out]
    d_attended = (
        jnp.einsum("td,ed->te", d_branch, out_full, preferred_element_type=jnp.float32)
        .astype(jnp.bfloat16)
        .reshape(row_count, HEADS, HEAD)
    )
    d_keys = jnp.zeros((row_count + WINDOW, HEAD), jnp.float32)
    d_values = jnp.zeros((row_count + WINDOW, HEAD), jnp.float32)
    query_grads = []
    for block_index in range(block_count):
        first_row = block_index * block_rows
        allowed = band_mask(first_row, block_rows, positions)
        query_block = query_rot[first_row : first_row + block_rows]
        key_block = keys_ext[first_row : first_row + key_span]
        value_block = values_ext[first_row : first_row + key_span]
        grad_block = d_attended[first_row : first_row + block_rows]
        scores = block_scores(query_block, key_block, allowed, scale)
        probs = jnp.where(allowed[None], jnp.exp(scores - log_sums[block_index]), 0.0)
        probs_low = probs.astype(jnp.bfloat16)
        d_values = d_values.at[first_row : first_row + key_span].add(
            jnp.einsum("hqk,qhd->kd", probs_low, grad_block, preferred_element_type=jnp.float32)
        )
        d_probs = jnp.einsum(
            "qhd,kd->hqk", grad_block, value_block, preferred_element_type=jnp.float32
        )
        centre = jnp.sum(probs * d_probs, axis=-1, keepdims=True)
        d_scores = (probs * (d_probs - centre)).astype(jnp.bfloat16)
        query_grads.append(
            jnp.einsum("hqk,kd->qhd", d_scores, key_block, preferred_element_type=jnp.float32)
            * scale
        )
        d_keys = d_keys.at[first_row : first_row + key_span].add(
            jnp.einsum("hqk,qhd->kd", d_scores, query_block, preferred_element_type=jnp.float32)
            * scale
        )
        query_grads[-1], d_attended = advance(sums, query_grads[-1], d_attended, times=2)
    back = passed_along(
        jnp.concatenate([d_keys[:WINDOW], d_values[:WINDOW]], axis=1).astype(jnp.bfloat16),
        ("seq", "fsdp"),
        -1,
    ).astype(jnp.float32)
    back = jnp.pad(back, ((tail_start, 0), (0, 0)))
    d_key = d_keys[WINDOW:] + back[:, :HEAD]
    d_value = d_values[WINDOW:] + back[:, HEAD:]
    d_query = jnp.concatenate(query_grads)
    turned_query = rotate(d_query, cosine[:, None, :], -sine[:, None, :])
    grad_scale_query = jnp.sum(turned_query * unit_query, axis=(0, 1))
    d_query_raw = (
        rms_back(unit_query, inv_query, turned_query * scale_query)
        .astype(jnp.bfloat16)
        .reshape(row_count, HEADS * HEAD)
    )
    turned_key = rotate(d_key, cosine, -sine)
    grad_scale_key = jnp.sum(turned_key * unit_key, axis=0)
    d_key_raw = rms_back(unit_key, inv_key, turned_key * scale_key).astype(jnp.bfloat16)
    d_value_raw = d_value.astype(jnp.bfloat16)
    d_query_raw = advance(sums, d_query_raw)
    d_raw = jnp.concatenate([d_query_raw, d_key_raw, d_value_raw], axis=1)
    grad_qkv = jnp.einsum("td,te->de", normed, d_raw, preferred_element_type=jnp.float32)
    low_qkv = grad_qkv.astype(jnp.bfloat16).reshape(count, rows_in, width)
    low_qkv, d_raw = advance(sums, low_qkv, d_raw)
    sum_query = reduce_rows(low_qkv[:, :, :wide], 1, True)
    d_normed = jnp.einsum("te,de->td", d_raw, qkv_full, preferred_element_type=jnp.float32)
    grad_scale_in = jnp.sum(d_normed * unit_in, axis=0)
    grad_tokens = d_middle + rms_back(unit_in, inv_in, d_normed * scale_in)
    terms = [grad_scale_in, grad_scale_query, grad_scale_key]
    terms += [grad_scale_attn, grad_scale_pre, grad_scale_ffn]
    terms = jnp.concatenate([item.reshape(count, -1) for item in terms], axis=1)
    terms = jnp.pad(terms[:, None], ((0, 0), (0, 15), (0, 2 * HEAD - terms.shape[1])))
    rest = jnp.concatenate([low_qkv[:, :, wide:], terms.astype(jnp.bfloat16)], axis=1)
    sum_rest = reduce_rows(rest, 1, False)
    sums += [sum_query, sum_rest]
    ends = [group.finish()[0].astype(jnp.float32) for group in sums]
    grad_down, grad_gate, grad_up, grad_out, grad_query, rest = ends
    grad_key = rest[:rows_in, :HEAD]
    grad_value = rest[:rows_in, HEAD:]
    gain_grads, at = [], 0
    for size in sizes:
        gain_grads.append(rest[rows_in, at : at + size])
        at += size
    return (
        output,
        grad_tokens,
        grad_query,
        grad_key,
        grad_value,
        grad_out,
        grad_gate,
        grad_up,
        grad_down,
        *gain_grads,
    )


def solution(mesh):
    in_specs = (
        P(("seq", "fsdp"), None),
        P(("seq", "fsdp")),
        P(("seq", "fsdp")),
        P("fsdp", None),
        P("fsdp", None),
        P("fsdp", None),
        P("fsdp", None),
        P("fsdp", None),
        P("fsdp", None),
        P("fsdp", None),
        P("fsdp"),
        P("fsdp"),
        P("fsdp"),
        P("fsdp"),
        P("fsdp"),
        P("fsdp"),
        P(("seq", "fsdp"), None),
    )
    out_specs = (
        P(("seq", "fsdp"), None),
        P(("seq", "fsdp"), None),
        P("fsdp", None),
        P("fsdp", None),
        P("fsdp", None),
        P("fsdp", None),
        P("fsdp", None),
        P("fsdp", None),
        P("fsdp", None),
        P("fsdp"),
        P("fsdp"),
        P("fsdp"),
        P("fsdp"),
        P("fsdp"),
        P("fsdp"),
    )
    return jax.shard_map(
        on_device, mesh=mesh, in_specs=in_specs, out_specs=out_specs, check_vma=False
    )
```
